512 devices in a mesh: dp: 32 (over z_lo, x, core), mp: 16 (over z_hi, y).
Axes of the slice: x: 4, y: 4, z: 16 (z_hi: 4, z_lo: 4; z = z_hi * 4 + z_lo), core: 2. Of those that a mesh axis runs over, the one named last changes fastest.
Arguments:
- grads: bfloat16 [32, 2, 256, 28672], P('dp', None, None, 'mp'), may hold values from -6 to 6
- weights: bfloat16 [2, 256, 28672], P(None, 'dp', 'mp'), may hold values from -1.5 to 1.5
- first_moment: float32 [2, 256, 256], P(None, 'dp'), may hold values from -6 to 6
- second_moment: float32 [2, 256, 256], P(None, 'dp'), may hold values from 1 to 16
- old_seeds: int32 [2], replicated, may hold values from 0 to 999999
- new_seeds: int32 [2], replicated, may hold values from 0 to 999999
Outputs:
- new_weights: bfloat16 [2, 256, 28672], P(None, None, 'mp')
- new_first: float32 [2, 256, 256], P(None, 'dp')
- new_second: float32 [2, 256, 256], P(None, 'dp')
The draws below stay inside these ranges and needn't reach their ends.
Inputs may be any that keep to these rules, and one draw needn't show every extreme that they name: `old_seeds`: seeds of the counter-based generator; old and new seeds are drawn independently. `new_seeds`: seeds of the counter-based generator; old and new seeds are drawn independently.
All inputs are finite; a program needn't handle non-finite values.
Results may differ from the reference program's by a relative error of at most 0.0053.
Values may be sent and summed in bfloat16 or wider, within the bound.
No kernel may reach another device: no remote copies, remote signals or barrier semaphores. Data moves between devices by JAX's collectives and lax.ppermute only.
A program may use at most 64 MiB of HBM per device.

```python
import math
import jax
import jax.numpy as jnp
from jax import lax

N = 28672
R = 256
LAYERS = 2
ROWS = 256
REPLICAS = 32


def raised(array, rng, source, target, parts, factor):
    def block_of(dim):
        return (jnp.arange(array.shape[dim]) // (array.shape[dim] // parts)).reshape((-1,) + (1,) * (array.ndim - 1 - dim))

    one_side = jax.random.permutation(rng, parts)[block_of(target)]
    other_side = (block_of(target) + parts // 2) % parts
    return jnp.where((block_of(source) == one_side) | (block_of(source) == other_side), factor * array, array)


def block_scale(rng, extent, pieces, smallest, high):
    def one(position, parts):
        heights = jax.random.uniform(jax.random.fold_in(jax.random.fold_in(rng, 6), position), (parts,), jnp.float32, smallest / len(pieces), high / len(pieces))
        return jnp.repeat(jnp.exp(heights), extent[position] // parts).reshape((-1,) + (1,) * (len(extent) - position - 1))

    gain = one(*pieces[0])
    for cut in pieces[1:]:
        gain = gain * one(*cut)
    return gain


def noise(key, dims, scale, bound, shards=(), kind=jnp.bfloat16):
    gain = block_scale(key, dims, shards, -0.22, 0.18) if shards else 1.0
    result = jax.random.normal(key, dims, jnp.float32) * scale * gain
    return jnp.minimum(jnp.maximum(result, -bound), bound).astype(kind)


def bell_draw_with(own_key, shape, width, most, cuts, heavy, kind=jnp.bfloat16):
    drawn = width * jax.random.normal(own_key, shape, jnp.float32)
    if cuts:
        drawn = drawn * block_scale(own_key, shape, cuts, -0.22, 0.18)
    return jnp.clip(raised(drawn, jax.random.fold_in(own_key, 3), *heavy), -most, most).astype(kind)


def setup_inputs(seed: int = 0) -> dict:
    streams_of = jax.random.split(jax.random.key(seed), 7)
    return {
        "grads": bell_draw_with(streams_of[0], (REPLICAS, LAYERS, ROWS, N), 1.0, 6.0, ((0, 32), (3, 16)), (0, 2, 32, 2.75)),
        "weights": noise(streams_of[1], (LAYERS, ROWS, N), 0.25, 1.5, ((1, 32), (2, 16))),
        "first_moment": noise(streams_of[2], (LAYERS, ROWS, R), 1.0, 6.0, ((1, 32),), jnp.float32),
        "second_moment": jnp.clip(jnp.exp(math.log(16.0) - 2.7725887 * jax.random.uniform(streams_of[3], (LAYERS, ROWS, R), jnp.float32) ** block_scale(streams_of[3], (LAYERS, ROWS, R), ((1, 32),), -0.2, 0.2)), 1.0, 16.0),
        "old_seeds": jax.random.randint(streams_of[4], (LAYERS,), 0, 1000000).astype(jnp.int32),
        "new_seeds": jax.random.randint(streams_of[5], (LAYERS,), 0, 1000000).astype(jnp.int32),
    }


def scramble(values):
    return (values % 46000 * (values // 2 % 46000 + 1) + 12345) % 65521

def generate(seed_value, rank_ids, columns):
    offset = seed_value % 65521
    row_key = (rank_ids * 251 + offset * 3) % 65521
    col_key = scramble((columns * 7 + offset) % 65521)
    hashed = scramble((row_key[:, None] + 2 * col_key[None, :]) % 65521)
    hashed = scramble((hashed * 3 + row_key[:, None]) % 65521)
    spread = math.sqrt(12.0 / rank_ids.shape[0])
    return ((hashed.astype(jnp.float32) + 0.5) / 65521.0 - 0.5) * spread

def reference(grads, weights, first_moment, second_moment, old_seeds, new_seeds):
    rank_ids = jnp.arange(R, dtype=jnp.int32)
    columns = jnp.arange(N, dtype=jnp.int32)
    weight_list = []
    first_list = []
    second_list = []
    for layer_id in range(LAYERS):
        old_proj = generate(old_seeds[layer_id], rank_ids, columns).astype(jnp.bfloat16)
        new_proj = generate(new_seeds[layer_id], rank_ids, columns).astype(jnp.bfloat16)
        gram_matrix = jnp.dot(old_proj, new_proj.T, preferred_element_type=jnp.float32)

        def accumulate(replica, total):
            return total + grads[replica, layer_id].astype(jnp.float32)
        summed = lax.fori_loop(0, REPLICAS, accumulate, jnp.zeros((ROWS, N), jnp.float32))
        compressed = jnp.dot(summed, new_proj.astype(jnp.float32).T, precision=lax.Precision.HIGHEST)
        moment = 0.9 * jnp.dot(first_moment[layer_id], gram_matrix, precision=lax.Precision.HIGHEST) + 0.1 * compressed
        second = 0.95 * jnp.dot(second_moment[layer_id], gram_matrix * gram_matrix, precision=lax.Precision.HIGHEST) + 0.05 * compressed * compressed
        direction = (moment / (jnp.sqrt(second) + 1e-08)).astype(jnp.bfloat16)
        update = jnp.dot(direction, new_proj, preferred_element_type=jnp.float32)
        weight_list.append((weights[layer_id].astype(jnp.float32) - 0.5 * update).astype(jnp.bfloat16))
        first_list.append(moment)
        second_list.append(second)
    return (jnp.stack(weight_list), jnp.stack(first_list), jnp.stack(second_list))
```

```python
import functools
import math

import jax
import jax.numpy as jnp
from jax import lax
from jax.experimental import pallas as pl
from jax.experimental.pallas import tpu as pltpu
from jax.sharding import PartitionSpec as P

PRIME = 65521
CUT = 46000
F32 = jnp.float32
BF16 = jnp.bfloat16
BOTH = ("dp", "mp")
NT = (((1,), (1,)), ((), ()))
TN = (((0,), (0,)), ((), ()))
HIGHEST = lax.Precision.HIGHEST


def device(z_lo, x, core, z_hi, y):
    return ((z_lo * 4 + x) * 2 + core) * 16 + z_hi * 4 + y


FOUR = range(4)
PLANES = [
    [device(z_lo, x, core, z_hi, y) for x in FOUR for y in FOUR for core in range(2)]
    for z_hi in FOUR
    for z_lo in FOUR
]
LINES = [
    [device(z_lo, x, core, z_hi, y) for z_hi in FOUR for z_lo in FOUR]
    for x in FOUR
    for y in FOUR
    for core in range(2)
]


def below(values, bound):
    return jnp.where(values >= bound, values - bound, values)


def fold(values):
    return values - PRIME * (values >> 16)


def product(values):
    return below(values, CUT) * ((values >> 1) + 1)


def scrambled(values):
    return below(fold(fold(product(values) + 12345)), PRIME)


def row_keys(offset, rank_ids):
    return below(fold(rank_ids * 251 + offset * 3), PRIME)


def column_keys(offset, columns):
    return below(2 * scrambled(below(fold(columns * 7 + offset), PRIME)), PRIME)


def entries(keys, keys_later, columns2, spread):
    first = fold(product(below(keys + columns2, PRIME)))
    second = below(fold(first * 3 + keys_later), PRIME)
    last = fold(product(second) + 12345).astype(F32)
    whole = jnp.floor((last + 0.5) * (1.0 / PRIME))
    return (((last - 32760.0) - whole * float(PRIME)) * (spread / PRIME)).astype(BF16)


def project_kernel(
    place, new_seeds, old_seeds, grads, proj, send, keys, columns2, old_rows, *, rank, cols, spread
):
    layer_id = pl.program_id(0)
    dp, mp = place[0], place[1]
    lanes = lax.broadcasted_iota(jnp.int32, (8, cols), 1) + mp * cols
    row = lax.broadcasted_iota(jnp.int32, (rank, 128), 0)
    tiles = cols // 128
    offset = lax.rem(new_seeds[layer_id], PRIME)
    keys[...] = row_keys(offset, row)
    columns2[...] = column_keys(offset, lanes)

    def wide(narrow):
        return jnp.concatenate([narrow] * tiles, axis=1)

    def both_halves(eight):
        return jnp.concatenate([eight, eight], axis=0)

    def chunk(index, _):
        at = pl.multiple_of(index * 16, 16)
        mine = keys[pl.ds(at, 16), :]
        later = below(mine + 3 * 12345, PRIME)
        for tile in range(tiles):
            cut = slice(tile * 128, tile * 128 + 128)
            proj[0, pl.ds(at, 16), cut] = entries(
                mine, later, both_halves(columns2[:, cut]), spread
            )
        return 0

    lax.fori_loop(0, rank // 16, chunk, 0)
    compressed = lax.dot_general(proj[0], grads[0, 0], NT, preferred_element_type=F32)
    send[:, 0:16, :] = compressed.astype(BF16).reshape(rank // 16, 16, rank)

    mine_layer = dp // (rank // 16)

    @pl.when(layer_id == mine_layer)
    def _():
        old_rows[...] = jnp.zeros_like(old_rows)
        old_offset = lax.rem(old_seeds[layer_id], PRIME)
        at = pl.multiple_of((dp % (rank // 16)) * 16, 16)
        mine = row_keys(old_offset, lax.broadcasted_iota(jnp.int32, (16, 128), 0) + at)
        later = below(mine + 3 * 12345, PRIME)
        columns2[...] = column_keys(old_offset, lanes)
        for tile in range(tiles):
            cut = slice(tile * 128, tile * 128 + 128)
            old_rows[pl.ds(at, 16), cut] = entries(
                mine, later, both_halves(columns2[:, cut]), spread
            )
        gram = lax.dot_general(proj[0], old_rows[...], NT, preferred_element_type=F32)
        send[:, 16:32, :] = gram.astype(BF16).reshape(rank // 16, 16, rank)

    @pl.when(layer_id != mine_layer)
    def _():
        send[:, 16:32, :] = jnp.zeros((rank // 16, 16, rank), BF16)


def sum_kernel(received, send):
    total = received[0].astype(F32)
    for part in range(1, received.shape[0]):
        total = total + received[part].astype(F32)
    send[...] = jnp.broadcast_to(total.astype(BF16)[None], send.shape)


def moment_kernel(place, received, first_moment, second_moment, send):
    z_lo = place[0] // 8
    total = received[0].astype(F32)
    for part in range(1, received.shape[0]):
        total = total + received[part].astype(F32)
    compressed, gram = total[0:16], total[16:32]
    first = (
        0.9
        * lax.dot_general(
            gram, first_moment[0].astype(F32), NT, precision=HIGHEST, preferred_element_type=F32
        )
        + 0.1 * compressed
    )
    second = (
        0.95
        * lax.dot_general(
            gram * gram,
            second_moment[0].astype(F32),
            NT,
            precision=HIGHEST,
            preferred_element_type=F32,
        )
        + 0.05 * compressed * compressed
    )
    direction = (first / (jnp.sqrt(second) + 1e-08)).astype(BF16)
    rows = lax.broadcasted_iota(jnp.int32, (256, 256), 0)
    lanes = lax.broadcasted_iota(jnp.int32, (256, 256), 1)
    picked = jnp.zeros((16, 256), F32)
    for slot, value in enumerate((first, second)):
        high = value.astype(BF16)
        low = (value - high.astype(F32)).astype(BF16)
        for base, part in ((64 * slot, high), (128 + 64 * slot, low)):
            lane = lanes - base
            chosen = (lane >= 0) & (lane < 64) & (rows == lane + 64 * z_lo)
            picked = picked + jnp.dot(
                part, jnp.where(chosen, 1.0, 0.0).astype(BF16), preferred_element_type=F32
            )
    send[:, 0:16, :] = jnp.broadcast_to(direction[None], (send.shape[0], 16, 256))
    send[:, 16:32, :] = jnp.broadcast_to(picked.astype(BF16)[None], (send.shape[0], 16, 256))


def update_kernel(place, received, proj, weights, new_weights, moments):
    direction = received[:, 0:16, :].reshape(256, 256)
    update = lax.dot_general(direction, proj[0], TN, preferred_element_type=F32)
    new_weights[0] = (weights[0].astype(F32) - 0.5 * update).astype(BF16)
    block = place[0] % 8
    rows = lax.broadcasted_iota(jnp.int32, (16, 256), 0)
    lanes = lax.broadcasted_iota(jnp.int32, (16, 256), 1)
    wanted = (rows // 8) * 64 + block * 8 + rows % 8
    chosen = jnp.where(lanes % 128 == wanted, 1.0, 0.0).astype(BF16)
    moments[0] = lax.dot_general(
        chosen, received[:, 16:32, :].reshape(256, 256), NT, preferred_element_type=F32
    )


def shards(grads, weights, first_moment, second_moment, old_seeds, new_seeds):
    layers, _, cols = weights.shape
    rank = first_moment.shape[2]
    half = rank // 16
    spread = math.sqrt(12.0 / rank)
    place = jnp.stack([lax.axis_index("dp"), lax.axis_index("mp")]).astype(jnp.int32)

    state = jnp.concatenate(
        [weights, first_moment.astype(BF16), second_moment.astype(BF16)], axis=2
    )
    state = lax.all_gather(state, "dp", axis=1, tiled=True)

    smem = pl.BlockSpec(memory_space=pltpu.SMEM)
    proj, send = pl.pallas_call(
        functools.partial(project_kernel, rank=rank, cols=cols, spread=spread),
        grid=(layers,),
        in_specs=[
            smem,
            smem,
            smem,
            pl.BlockSpec((1, 1, rank, cols), lambda layer: (0, layer, 0, 0)),
        ],
        out_specs=[
            pl.BlockSpec((1, rank, cols), lambda layer: (layer, 0, 0)),
            pl.BlockSpec((half, 32, rank), lambda layer: (layer, 0, 0)),
        ],
        out_shape=[
            jax.ShapeDtypeStruct((layers, rank, cols), BF16),
            jax.ShapeDtypeStruct((layers * half, 32, rank), BF16),
        ],
        scratch_shapes=[
            pltpu.VMEM((rank, 128), jnp.int32),
            pltpu.VMEM((8, cols), jnp.int32),
            pltpu.VMEM((rank, cols), BF16),
        ],
        compiler_params=pltpu.CompilerParams(vmem_limit_bytes=32 * 2**20),
        name="project",
    )(place, new_seeds, old_seeds, grads)

    received = lax.all_to_all(send, BOTH, 0, 0, axis_index_groups=PLANES, tiled=True)
    send = pl.pallas_call(
        sum_kernel,
        out_shape=jax.ShapeDtypeStruct((16, 32, rank), BF16),
        name="plane_sum",
    )(received)
    received = lax.all_to_all(send, BOTH, 0, 0, axis_index_groups=LINES, tiled=True)

    dp, mp = place[0], place[1]
    x_core, y = dp % 8, mp % 4
    owner = ((x_core // 2) * 4 + y) * 2 + x_core % 2
    place = jnp.stack([dp, mp, owner // half])
    send = pl.pallas_call(
        moment_kernel,
        grid_spec=pltpu.PrefetchScalarGridSpec(
            num_scalar_prefetch=1,
            grid=(1,),
            in_specs=[
                pl.BlockSpec((16, 32, rank), lambda _, where: (0, 0, 0)),
                pl.BlockSpec((1, rank, rank), lambda _, where: (where[2], 0, cols // rank)),
                pl.BlockSpec((1, rank, rank), lambda _, where: (where[2], 0, cols // rank + 1)),
            ],
            out_specs=pl.BlockSpec((32, 32, rank), lambda _, where: (0, 0, 0)),
        ),
        out_shape=jax.ShapeDtypeStruct((32, 32, rank), BF16),
        name="moment",
    )(place, received, state, state)
    received = lax.all_to_all(send, BOTH, 0, 0, axis_index_groups=PLANES, tiled=True)

    new_weights, moments = pl.pallas_call(
        update_kernel,
        grid=(layers,),
        in_specs=[
            smem,
            pl.BlockSpec((half, 32, rank), lambda layer: (layer, 0, 0)),
            pl.BlockSpec((1, rank, cols), lambda layer: (layer, 0, 0)),
            pl.BlockSpec((1, rank, cols), lambda layer: (layer, 0, 0)),
        ],
        out_specs=[
            pl.BlockSpec((1, rank, cols), lambda layer: (layer, 0, 0)),
            pl.BlockSpec((1, 16, rank), lambda layer: (layer, 0, 0)),
        ],
        out_shape=[
            jax.ShapeDtypeStruct((layers, rank, cols), BF16),
            jax.ShapeDtypeStruct((layers, 16, rank), F32),
        ],
        compiler_params=pltpu.CompilerParams(vmem_limit_bytes=32 * 2**20),
        name="update",
    )(place, received, proj, state)
    return new_weights, moments[:, 0:8], moments[:, 8:16]


def solution(mesh):
    placed = (
        P("dp", None, None, "mp"),
        P(None, "dp", "mp"),
        P(None, "dp", None),
        P(None, "dp", None),
        P(),
        P(),
    )
    return jax.shard_map(
        shards,
        mesh=mesh,
        in_specs=placed,
        out_specs=(P(None, None, "mp"), P(None, "dp", None), P(None, "dp", None)),
        check_vma=False,
    )
```

```python
import functools
import math

import jax
import jax.numpy as jnp
from jax import lax
from jax.experimental import pallas as pl
from jax.experimental.pallas import tpu as pltpu
from jax.sharding import PartitionSpec as P

PRIME = 65521
CUT = 46000
F32 = jnp.float32
BF16 = jnp.bfloat16
BOTH = ("dp", "mp")
NT = (((1,), (1,)), ((), ()))
TN = (((0,), (0,)), ((), ()))
HIGHEST = lax.Precision.HIGHEST


FOUR = range(4)
TWO = range(2)


def device(z, x, core, y):
    return ((z % 4 * 4 + x) * 2 + core) * 16 + z // 4 * 4 + y


SLABS = [
    [device(2 * pair + odd, x, core, y) for odd in TWO for x in FOUR for y in FOUR for core in TWO]
    for pair in range(8)
]
LINES = [
    [device(2 * pair + odd, x, core, y) for pair in range(8)]
    for odd in TWO
    for x in FOUR
    for y in FOUR
    for core in TWO
]


def copy_index(z_lo, x, core):
    return (z_lo * 4 + x) * 2 + core


def swap(z, x, core):
    return [
        (copy_index(a, b, c), copy_index(a ^ z, b ^ x, c ^ core))
        for a in FOUR
        for b in FOUR
        for c in TWO
    ]


def below(values, bound):
    return jnp.where(values >= bound, values - bound, values)


def fold(values):
    return values - PRIME * (values >> 16)


def product(values):
    return below(values, CUT) * ((values >> 1) + 1)


def scrambled(values):
    return below(fold(fold(product(values) + 12345)), PRIME)


def row_keys(offset, rank_ids):
    return below(fold(rank_ids * 251 + offset * 3), PRIME)


def column_keys(offset, columns):
    return below(2 * scrambled(below(fold(columns * 7 + offset), PRIME)), PRIME)


def entries(keys, keys_later, columns2, spread):
    first = fold(product(below(keys + columns2, PRIME)))
    second = below(fold(first * 3 + keys_later), PRIME)
    last = fold(product(second) + 12345).astype(F32)
    whole = jnp.floor((last + 0.5) * (1.0 / PRIME))
    return (((last - 32760.0) - whole * float(PRIME)) * (spread / PRIME)).astype(BF16)


def project_kernel(
    place,
    grads_hbm,
    first_moment,
    second_moment,
    weights,
    proj_hbm,
    send,
    weights_out,
    grads,
    proj,
    keys,
    columns2,
    old_rows,
    load_sems,
    store_sems,
    *,
    spread,
):
    layers, rank, cols = proj.shape
    dp, mp = place[0], place[1]
    tiles = cols // 128
    share = 64 // layers
    loads = [
        pltpu.make_async_copy(grads_hbm.at[0, layer], grads.at[layer], load_sems.at[layer])
        for layer in range(layers)
    ]
    stores = [
        pltpu.make_async_copy(proj.at[layer], proj_hbm.at[layer], store_sems.at[layer])
        for layer in range(layers)
    ]
    for load in loads:
        load.start()
    weights_out[...] = weights[...]
    lanes = lax.broadcasted_iota(jnp.int32, (8, cols), 1) + mp * cols
    row = lax.broadcasted_iota(jnp.int32, (rank, 128), 0)

    def both_halves(eight):
        return jnp.concatenate([eight, eight], axis=0)

    y = mp % 4
    for layer in range(layers):
        group = slice(share * layer, share * layer + share)
        offset = lax.rem(place[2 + layer], PRIME)
        keys[...] = row_keys(offset, row)
        columns2[...] = column_keys(offset, lanes)

        def chunk(index, _, layer=layer):
            at = pl.multiple_of(index * 16, 16)
            mine = keys[pl.ds(at, 16), :]
            later = below(mine + 3 * 12345, PRIME)
            for tile in range(tiles):
                cut = slice(tile * 128, tile * 128 + 128)
                proj[layer, pl.ds(at, 16), cut] = entries(
                    mine, later, both_halves(columns2[:, cut]), spread
                )
            return 0

        lax.fori_loop(0, rank // 16, chunk, 0)
        stores[layer].start()
        loads[layer].wait()
        compressed = lax.dot_general(proj[layer], grads[layer], NT, preferred_element_type=F32)
        send[group, :, 0:rank] = compressed.reshape(share, 8, rank).astype(BF16)
        moments = jnp.where(y < 2, first_moment[layer], second_moment[layer])
        half = jnp.where(y % 2 == 0, moments[:, 0:128], moments[:, 128:256])
        send[group, :, 2 * rank : 2 * rank + 128] = jnp.broadcast_to(
            half[None], (share, 8, 128)
        ).astype(BF16)

        mine_layer = dp // (rank // 16)

        @pl.when(mine_layer == layer)
        def _(layer=layer, group=group):
            old_rows[...] = jnp.zeros_like(old_rows)
            old_offset = lax.rem(place[4 + layer], PRIME)
            at = pl.multiple_of((dp % (rank // 16)) * 16, 16)
            mine = row_keys(old_offset, lax.broadcasted_iota(jnp.int32, (16, 128), 0) + at)
            later = below(mine + 3 * 12345, PRIME)
            columns2[...] = column_keys(old_offset, lanes)
            for tile in range(tiles):
                cut = slice(tile * 128, tile * 128 + 128)
                old_rows[pl.ds(at, 16), cut] = entries(
                    mine, later, both_halves(columns2[:, cut]), spread
                )
            gram = lax.dot_general(proj[layer], old_rows[...], NT, preferred_element_type=F32)
            send[group, :, rank : 2 * rank] = gram.reshape(share, 8, rank).astype(BF16)

        @pl.when(mine_layer != layer)
        def _(group=group):
            send[group, :, rank : 2 * rank] = jnp.zeros((share, 8, rank), BF16)

    for store in stores:
        store.wait()


def summed(received, width):
    total = received[0, :, 0:width].astype(F32)
    for part in range(1, received.shape[0]):
        total = total + received[part, :, 0:width].astype(F32)
    return total


def sum_kernel(received, send, moments):
    send[...] = jnp.broadcast_to(summed(received, 512)[None], send.shape).astype(BF16)
    for chip in range(8):
        for y in FOUR:
            from_core = [received[(chip * 4 + y) * 2 + core, :, 512:640].astype(F32) for core in TWO]
            lanes = slice(y % 2 * 128, y % 2 * 128 + 128)
            moments[y // 2, chip * 16 : chip * 16 + 16, lanes] = jnp.concatenate(
                from_core, axis=0
            ).astype(BF16)


def join_kernel(*refs):
    *pieces, _, joined = refs
    for slot, piece in enumerate(pieces):
        joined[slot] = piece[...]


def moment_kernel(place, received, near, far, *refs):
    send = refs[-1]
    total = summed(received, 512)
    compressed, gram = total[:, 0:256], total[:, 256:512]
    upper = (place[0] // 16) == 1

    def times(left, which):
        near_part, far_part = near[which].astype(F32), far[which].astype(F32)
        return jnp.concatenate(
            [
                lax.dot_general(
                    left, rows, NT, precision=HIGHEST, preferred_element_type=F32
                )
                for rows in (
                    jnp.where(upper, far_part, near_part),
                    jnp.where(upper, near_part, far_part),
                )
            ],
            axis=1,
        )

    first = 0.9 * times(gram, 0) + 0.1 * compressed
    second = 0.95 * times(gram * gram, 1) + 0.05 * compressed * compressed
    direction = first / (jnp.sqrt(second) + 1e-08)
    send[:, :, 0:256] = jnp.broadcast_to(direction[None], (64, 8, 256)).astype(BF16)
    mine = [jnp.where(upper, value[:, 128:256], value[:, 0:128]) for value in (first, second)]
    high = [value.astype(BF16).astype(F32) for value in mine]
    parts = high + [value - top for value, top in zip(mine, high)]
    lane = lax.broadcasted_iota(jnp.int32, (8, 128), 1)
    for quarter in FOUR:
        packed = pltpu.roll(parts[0], (128 - 32 * quarter) % 128, 1)
        for slot in (1, 2, 3):
            moved = pltpu.roll(parts[slot], (32 * slot - 32 * quarter) % 128, 1)
            packed = jnp.where(lane >= 32 * slot, moved, packed)
        send[16 * quarter : 16 * quarter + 16, :, 256:384] = jnp.broadcast_to(
            packed[None], (16, 8, 128)
        ).astype(BF16)


def update_kernel(place, received, proj, *refs):
    own, other = refs[0:4], refs[4:8]
    new_weights, new_first, new_second, update = refs[8:]
    dp = place[0]
    z, x, core = dp // 8, dp // 2 % 4, dp % 2
    cols = proj.shape[2]
    direction = received[:, :, 0:256].astype(F32).reshape(256, 256).astype(BF16)
    update[...] = 0.5 * lax.dot_general(direction, proj[0], TN, preferred_element_type=F32)
    for x_bits in FOUR:
        for z_bits in FOUR:
            at = pl.multiple_of((z ^ z_bits) * 64 + (x ^ x_bits) * 16, 16)
            mine = own[x_bits][z_bits, 0].astype(F32)
            theirs = other[x_bits][z_bits, 0].astype(F32)
            low = jnp.where(core == 0, mine, theirs)
            high = jnp.where(core == 0, theirs, mine)
            block = jnp.concatenate([low, high], axis=0)
            new_weights[0, pl.ds(at, 16), :] = (block - update[pl.ds(at, 16), :]).astype(BF16)
    rows = lax.broadcasted_iota(jnp.int32, (16, 128), 0)
    lanes = lax.broadcasted_iota(jnp.int32, (16, 128), 1)
    wanted = rows // 8 * 32 + x % 2 * 16 + core * 8 + rows % 8
    chosen = jnp.where(lanes % 64 == wanted, 1.0, 0.0).astype(BF16)
    moments = lax.dot_general(
        chosen,
        received[:, :, 256:384].astype(F32).reshape(256, 128).astype(BF16),
        NT,
        preferred_element_type=F32,
    )
    new_first[0] = moments[0:8]
    new_second[0] = moments[8:16]


def shards(grads, weights, first_moment, second_moment, old_seeds, new_seeds):
    layers, block, cols = weights.shape
    rank = first_moment.shape[2]
    spread = math.sqrt(12.0 / rank)
    place = jnp.concatenate(
        [jnp.stack([lax.axis_index("dp"), lax.axis_index("mp")]).astype(jnp.int32), new_seeds, old_seeds]
    )
    smem = pl.BlockSpec(memory_space=pltpu.SMEM)
    vmem = pl.BlockSpec(memory_space=pltpu.VMEM)
    hbm = pl.BlockSpec(memory_space=pltpu.HBM)
    anywhere = pl.BlockSpec(memory_space=pl.ANY)
    roomy = pltpu.CompilerParams(vmem_limit_bytes=56 * 2**20)
    small = pltpu.CompilerParams(vmem_limit_bytes=8 * 2**20)

    proj, send, weights = pl.pallas_call(
        functools.partial(project_kernel, spread=spread),
        in_specs=[smem, hbm, vmem, vmem, vmem],
        out_specs=[hbm, vmem, vmem],
        out_shape=[
            jax.ShapeDtypeStruct((layers, rank, cols), BF16),
            jax.ShapeDtypeStruct((64, 8, 640), BF16),
            jax.ShapeDtypeStruct(weights.shape, BF16),
        ],
        scratch_shapes=[
            pltpu.VMEM((layers, rank, cols), BF16),
            pltpu.VMEM((layers, rank, cols), BF16),
            pltpu.VMEM((rank, 128), jnp.int32),
            pltpu.VMEM((8, cols), jnp.int32),
            pltpu.VMEM((rank, cols), BF16),
            pltpu.SemaphoreType.DMA((layers,)),
            pltpu.SemaphoreType.DMA((layers,)),
        ],
        compiler_params=roomy,
        cost_estimate=pl.CostEstimate(
            flops=8 * 10**9, bytes_accessed=6 * 10**6, transcendentals=0
        ),
        name="project",
    )(place, grads, first_moment, second_moment, weights)

    received = lax.all_to_all(send, BOTH, 0, 0, axis_index_groups=SLABS, tiled=True)
    column = [weights] + [lax.ppermute(weights, "dp", swap(bits, 0, 0)) for bits in (1, 2, 3)]
    send, near = pl.pallas_call(
        sum_kernel,
        in_specs=[vmem],
        out_specs=[vmem, vmem],
        out_shape=[
            jax.ShapeDtypeStruct((8, 8, 2 * rank), BF16),
            jax.ShapeDtypeStruct((2, rank // 2, rank), BF16),
        ],
        compiler_params=small,
        name="slab_sum",
    )(received)
    received = lax.all_to_all(send, BOTH, 0, 0, axis_index_groups=LINES, tiled=True)
    far = lax.ppermute(near, "dp", swap(2, 0, 0))
    column = pl.pallas_call(
        join_kernel,
        in_specs=[vmem] * 4 + [anywhere],
        out_specs=vmem,
        out_shape=jax.ShapeDtypeStruct((4, *weights.shape), BF16),
        compiler_params=small,
        name="join",
    )(*column, near)
    own = [column] + [lax.ppermute(column, "dp", swap(0, bits, 0)) for bits in (1, 2, 3)]
    send = pl.pallas_call(
        moment_kernel,
        in_specs=[smem, vmem, vmem, vmem] + [anywhere] * 3,
        out_specs=vmem,
        out_shape=jax.ShapeDtypeStruct((64, 8, 384), BF16),
        compiler_params=small,
        name="moment",
    )(place, received, near, far, *own[1:])
    received = lax.all_to_all(send, BOTH, 0, 0, axis_index_groups=SLABS, tiled=True)
    other = [lax.ppermute(piece, "dp", swap(0, 0, 1)) for piece in own]

    whole = pl.BlockSpec((1, rank, cols), lambda layer: (layer, 0, 0))
    piece = pl.BlockSpec((4, 1, block, cols), lambda layer: (0, layer, 0, 0))
    rows = pl.BlockSpec((1, block, rank), lambda layer: (layer, 0, 0))
    return pl.pallas_call(
        update_kernel,
        grid=(layers,),
        in_specs=[
            smem,
            pl.BlockSpec((64 // layers, 8, 384), lambda layer: (layer, 0, 0)),
            whole,
        ]
        + [piece] * 8,
        out_specs=[whole, rows, rows],
        out_shape=[
            jax.ShapeDtypeStruct((layers, rank, cols), BF16),
            jax.ShapeDtypeStruct((layers, block, rank), F32),
            jax.ShapeDtypeStruct((layers, block, rank), F32),
        ],
        scratch_shapes=[pltpu.VMEM((rank, cols), F32)],
        compiler_params=pltpu.CompilerParams(vmem_limit_bytes=56 * 2**20),
        name="update",
    )(place, received, proj, *own, *other)


def solution(mesh):
    placed = (
        P("dp", None, None, "mp"),
        P(None, "dp", "mp"),
        P(None, "dp", None),
        P(None, "dp", None),
        P(),
        P(),
    )
    return jax.shard_map(
        shards,
        mesh=mesh,
        in_specs=placed,
        out_specs=(P(None, None, "mp"), P(None, "dp", None), P(None, "dp", None)),
        check_vma=False,
    )
```

```python
import functools
import math

import jax
import jax.numpy as jnp
from jax import lax
from jax.experimental import pallas as pl
from jax.experimental.pallas import tpu as pltpu
from jax.sharding import PartitionSpec as P

PRIME = 65521
CUT = 46000
F32 = jnp.float32
BF16 = jnp.bfloat16
BOTH = ("dp", "mp")
NT = (((1,), (1,)), ((), ()))
TN = (((0,), (0,)), ((), ()))
HIGHEST = lax.Precision.HIGHEST


FOUR = range(4)
TWO = range(2)


def device(z, x, core, y):
    return ((z % 4 * 4 + x) * 2 + core) * 16 + z // 4 * 4 + y


SLABS = [
    [device(2 * pair + odd, x, core, y) for odd in TWO for x in FOUR for y in FOUR for core in TWO]
    for pair in range(8)
]
LINES = [
    [device(2 * pair + odd, x, core, y) for pair in range(8)]
    for odd in TWO
    for x in FOUR
    for y in FOUR
    for core in TWO
]


def copy_index(z_lo, x, core):
    return (z_lo * 4 + x) * 2 + core


def swap(z, x, core):
    return [
        (copy_index(a, b, c), copy_index(a ^ z, b ^ x, c ^ core))
        for a in FOUR
        for b in FOUR
        for c in TWO
    ]


def below(values, bound):
    return jnp.where(values >= bound, values - bound, values)


def fold(values):
    return values - PRIME * (values >> 16)


def product(values):
    return below(values, CUT) * ((values >> 1) + 1)


def scrambled(values):
    return below(fold(fold(product(values) + 12345)), PRIME)


def row_keys(offset, rank_ids):
    return below(fold(rank_ids * 251 + offset * 3), PRIME)


def column_keys(offset, columns):
    return below(2 * scrambled(below(fold(columns * 7 + offset), PRIME)), PRIME)


def entries(keys, keys_later, columns2, spread):
    first = fold(product(below(keys + columns2, PRIME)))
    second = below(fold(first * 3 + keys_later), PRIME)
    last = fold(product(second) + 12345).astype(F32)
    whole = jnp.floor((last + 0.5) * (1.0 / PRIME))
    return (((last - 32760.0) - whole * float(PRIME)) * (spread / PRIME)).astype(BF16)


def project_kernel(
    seeds,
    old_seeds,
    grads_hbm,
    first_hbm,
    second_hbm,
    weights_hbm,
    proj_hbm,
    send,
    weights_out,
    grads,
    moments,
    proj,
    keys,
    keys_later,
    columns2,
    old_rows,
    grads_sems,
    moment_sems,
    weights_sem,
    proj_sems,
    *,
    spread,
):
    layers, rank, cols = proj.shape
    dp, mp = lax.axis_index("dp"), lax.axis_index("mp")
    tiles = cols // 128
    share = 64 // layers
    grads_in = [
        pltpu.make_async_copy(grads_hbm.at[0, layer], grads.at[layer], grads_sems.at[layer])
        for layer in range(layers)
    ]
    moments_in = [
        pltpu.make_async_copy(source, moments.at[which], moment_sems.at[which])
        for which, source in enumerate((first_hbm, second_hbm))
    ]
    weights_move = pltpu.make_async_copy(weights_hbm, weights_out, weights_sem)
    proj_out = [
        pltpu.make_async_copy(proj.at[layer], proj_hbm.at[layer], proj_sems.at[layer])
        for layer in range(layers)
    ]
    for copy in (*grads_in, *moments_in, weights_move):
        copy.start()

    def both_halves(eight):
        return jnp.concatenate([eight, eight], axis=0)

    lanes = lax.broadcasted_iota(jnp.int32, (8, cols), 1) + mp * cols
    row = lax.broadcasted_iota(jnp.int32, (rank, 128), 0)
    old_block = dp % (rank // 16)
    old_row = lax.broadcasted_iota(jnp.int32, (16, 128), 0) + old_block * 16
    for layer in range(layers):
        offset = lax.rem(old_seeds[layer], PRIME)
        mine = row_keys(offset, old_row)
        later = below(mine + 3 * 12345, PRIME)
        old_columns2 = column_keys(offset, lanes)
        for tile in range(tiles):
            cut = slice(tile * 128, tile * 128 + 128)
            old_rows[layer, :, cut] = entries(
                mine, later, both_halves(old_columns2[:, cut]), spread
            )
        offset = lax.rem(seeds[layer], PRIME)
        keys[layer] = row_keys(offset, row)
        keys_later[layer] = below(keys[layer] + 3 * 12345, PRIME)
        columns2[layer] = column_keys(offset, lanes)

    for layer in range(layers):

        def chunk(index, _, layer=layer):
            rows = pl.ds(pl.multiple_of(index * 16, 16), 16)
            mine, later = keys[layer, rows, :], keys_later[layer, rows, :]
            for tile in range(tiles):
                cut = slice(tile * 128, tile * 128 + 128)
                proj[layer, rows, cut] = entries(
                    mine, later, both_halves(columns2[layer, :, cut]), spread
                )
            return 0

        lax.fori_loop(0, rank // 16, chunk, 0, unroll=2)
        proj_out[layer].start()

    for copy in (*grads_in, *moments_in):
        copy.wait()
    y = mp % 4
    spot_row = lax.broadcasted_iota(jnp.int32, (16, rank), 0) + old_block * 16
    spot_lane = lax.broadcasted_iota(jnp.int32, (16, rank), 1)
    for layer in range(layers):
        group = slice(share * layer, share * layer + share)
        compressed = lax.dot_general(proj[layer], grads[layer], NT, preferred_element_type=F32)
        send[group, :, 0:rank] = compressed.reshape(share, 8, rank).astype(BF16)
        gram = lax.dot_general(proj[layer], old_rows[layer], NT, preferred_element_type=F32)
        mine_layer = dp // (rank // 16) == layer
        spot = jnp.where((spot_row == spot_lane) & mine_layer, 1.0, 0.0).astype(BF16)
        placed = jnp.dot(gram.astype(BF16), spot, preferred_element_type=F32)
        send[group, :, rank : 2 * rank] = placed.reshape(share, 8, rank).astype(BF16)
        moment = jnp.where(y < 2, moments[0, layer], moments[1, layer])
        half = jnp.where(y % 2 == 0, moment[:, 0:128], moment[:, 128:256])
        send[group, :, 2 * rank : 2 * rank + 128] = jnp.broadcast_to(
            half[None], (share, 8, 128)
        ).astype(BF16)
    for copy in (weights_move, *proj_out):
        copy.wait()


def summed(received, width):
    total = received[0, :, 0:width].astype(F32)
    for part in range(1, received.shape[0]):
        total = total + received[part, :, 0:width].astype(F32)
    return total


def sum_kernel(received, send, moments):
    send[...] = jnp.broadcast_to(summed(received, 512)[None], send.shape).astype(BF16)
    for chip in range(8):
        for y in FOUR:
            from_core = [received[(chip * 4 + y) * 2 + core, :, 512:640].astype(F32) for core in TWO]
            lanes = slice(y % 2 * 128, y % 2 * 128 + 128)
            moments[y // 2, chip * 16 : chip * 16 + 16, lanes] = jnp.concatenate(
                from_core, axis=0
            ).astype(BF16)


def join_kernel(*refs):
    *pieces, _, joined = refs
    for slot, piece in enumerate(pieces):
        joined[slot] = piece[...]


def moment_kernel(received, near, far, *refs):
    send = refs[-1]
    total = summed(received, 512)
    compressed, gram = total[:, 0:256], total[:, 256:512]
    upper = (lax.axis_index("dp") // 16) == 1

    def times(left, which):
        near_part, far_part = near[which].astype(F32), far[which].astype(F32)
        return jnp.concatenate(
            [
                lax.dot_general(
                    left, rows, NT, precision=HIGHEST, preferred_element_type=F32
                )
                for rows in (
                    jnp.where(upper, far_part, near_part),
                    jnp.where(upper, near_part, far_part),
                )
            ],
            axis=1,
        )

    first = 0.9 * times(gram, 0) + 0.1 * compressed
    second = 0.95 * times(gram * gram, 1) + 0.05 * compressed * compressed
    direction = first / (jnp.sqrt(second) + 1e-08)
    send[:, :, 0:256] = jnp.broadcast_to(direction[None], (64, 8, 256)).astype(BF16)
    mine = [jnp.where(upper, value[:, 128:256], value[:, 0:128]) for value in (first, second)]
    high = [value.astype(BF16).astype(F32) for value in mine]
    parts = high + [value - top for value, top in zip(mine, high)]
    lane = lax.broadcasted_iota(jnp.int32, (8, 128), 1)
    for quarter in FOUR:
        packed = pltpu.roll(parts[0], (128 - 32 * quarter) % 128, 1)
        for slot in (1, 2, 3):
            moved = pltpu.roll(parts[slot], (32 * slot - 32 * quarter) % 128, 1)
            packed = jnp.where(lane >= 32 * slot, moved, packed)
        send[16 * quarter : 16 * quarter + 16, :, 256:384] = jnp.broadcast_to(
            packed[None], (16, 8, 128)
        ).astype(BF16)


def update_kernel(received, proj, *refs):
    own, other = refs[0:4], refs[4:8]
    new_weights, new_first, new_second, update = refs[8:]
    dp = lax.axis_index("dp")
    z, x, core = dp // 8, dp // 2 % 4, dp % 2
    direction = received[:, :, 0:256].astype(F32).reshape(256, 256).astype(BF16)
    update[...] = 0.5 * lax.dot_general(direction, proj[0], TN, preferred_element_type=F32)
    for x_bits in FOUR:
        for z_bits in FOUR:
            at = pl.multiple_of((z ^ z_bits) * 64 + (x ^ x_bits) * 16, 16)
            mine = own[x_bits][z_bits, 0].astype(F32)
            theirs = other[x_bits][z_bits, 0].astype(F32)
            low = jnp.where(core == 0, mine, theirs)
            high = jnp.where(core == 0, theirs, mine)
            block = jnp.concatenate([low, high], axis=0)
            new_weights[0, pl.ds(at, 16), :] = (block - update[pl.ds(at, 16), :]).astype(BF16)
    rows = lax.broadcasted_iota(jnp.int32, (16, 128), 0)
    lanes = lax.broadcasted_iota(jnp.int32, (16, 128), 1)
    wanted = rows // 8 * 32 + x % 2 * 16 + core * 8 + rows % 8
    chosen = jnp.where(lanes % 64 == wanted, 1.0, 0.0).astype(BF16)
    moments = lax.dot_general(
        chosen,
        received[:, :, 256:384].astype(F32).reshape(256, 128).astype(BF16),
        NT,
        preferred_element_type=F32,
    )
    new_first[0] = moments[0:8]
    new_second[0] = moments[8:16]


def shards(grads, weights, first_moment, second_moment, old_seeds, new_seeds):
    layers, block, cols = weights.shape
    rank = first_moment.shape[2]
    spread = math.sqrt(12.0 / rank)
    smem = pl.BlockSpec(memory_space=pltpu.SMEM)
    vmem = pl.BlockSpec(memory_space=pltpu.VMEM)
    hbm = pl.BlockSpec(memory_space=pltpu.HBM)
    anywhere = pl.BlockSpec(memory_space=pl.ANY)
    roomy = pltpu.CompilerParams(vmem_limit_bytes=251 * 2**18)
    small = pltpu.CompilerParams(vmem_limit_bytes=8 * 2**20)

    proj, send, weights = pl.pallas_call(
        functools.partial(project_kernel, spread=spread),
        in_specs=[smem, smem, hbm, hbm, hbm, hbm],
        out_specs=[hbm, vmem, hbm],
        out_shape=[
            jax.ShapeDtypeStruct((layers, rank, cols), BF16),
            jax.ShapeDtypeStruct((64, 8, 640), BF16),
            jax.ShapeDtypeStruct(weights.shape, BF16),
        ],
        scratch_shapes=[
            pltpu.VMEM((layers, rank, cols), BF16),
            pltpu.VMEM((2, layers, block, rank), F32),
            pltpu.VMEM((layers, rank, cols), BF16),
            pltpu.VMEM((layers, rank, 128), jnp.int32),
            pltpu.VMEM((layers, rank, 128), jnp.int32),
            pltpu.VMEM((layers, 8, cols), jnp.int32),
            pltpu.VMEM((layers, 16, cols), BF16),
            pltpu.SemaphoreType.DMA((layers,)),
            pltpu.SemaphoreType.DMA((2,)),
            pltpu.SemaphoreType.DMA(()),
            pltpu.SemaphoreType.DMA((layers,)),
        ],
        compiler_params=roomy,
        cost_estimate=pl.CostEstimate(
            flops=8 * 10**9, bytes_accessed=6 * 10**6, transcendentals=0
        ),
        name="project",
    )(new_seeds, old_seeds, grads, first_moment, second_moment, weights)

    received = lax.all_to_all(send, BOTH, 0, 0, axis_index_groups=SLABS, tiled=True)
    column = [weights] + [lax.ppermute(weights, "dp", swap(bits, 0, 0)) for bits in (1, 2, 3)]
    send, near = pl.pallas_call(
        sum_kernel,
        in_specs=[vmem],
        out_specs=[vmem, vmem],
        out_shape=[
            jax.ShapeDtypeStruct((8, 8, 2 * rank), BF16),
            jax.ShapeDtypeStruct((2, rank // 2, rank), BF16),
        ],
        compiler_params=small,
        name="slab_sum",
    )(received)
    received = lax.all_to_all(send, BOTH, 0, 0, axis_index_groups=LINES, tiled=True)
    far = lax.ppermute(near, "dp", swap(2, 0, 0))
    column = pl.pallas_call(
        join_kernel,
        in_specs=[vmem] * 4 + [anywhere],
        out_specs=vmem,
        out_shape=jax.ShapeDtypeStruct((4, *weights.shape), BF16),
        compiler_params=small,
        name="join",
    )(*column, near)
    own = [column] + [lax.ppermute(column, "dp", swap(0, bits, 0)) for bits in (1, 2, 3)]
    send = pl.pallas_call(
        moment_kernel,
        in_specs=[vmem, vmem, vmem] + [anywhere] * 3,
        out_specs=vmem,
        out_shape=jax.ShapeDtypeStruct((64, 8, 384), BF16),
        compiler_params=small,
        name="moment",
    )(received, near, far, *own[1:])
    received = lax.all_to_all(send, BOTH, 0, 0, axis_index_groups=SLABS, tiled=True)
    other = [lax.ppermute(piece, "dp", swap(0, 0, 1)) for piece in own]

    whole = pl.BlockSpec((1, rank, cols), lambda layer: (layer, 0, 0))
    piece = pl.BlockSpec((4, 1, block, cols), lambda layer: (0, layer, 0, 0))
    rows = pl.BlockSpec((1, block, rank), lambda layer: (layer, 0, 0))
    return pl.pallas_call(
        update_kernel,
        grid=(layers,),
        in_specs=[
            pl.BlockSpec((64 // layers, 8, 384), lambda layer: (layer, 0, 0)),
            whole,
        ]
        + [piece] * 8,
        out_specs=[whole, rows, rows],
        out_shape=[
            jax.ShapeDtypeStruct((layers, rank, cols), BF16),
            jax.ShapeDtypeStruct((layers, block, rank), F32),
            jax.ShapeDtypeStruct((layers, block, rank), F32),
        ],
        scratch_shapes=[pltpu.VMEM((rank, cols), F32)],
        compiler_params=roomy,
        name="update",
    )(received, proj, *own, *other)


def solution(mesh):
    placed = (
        P("dp", None, None, "mp"),
        P(None, "dp", "mp"),
        P(None, "dp", None),
        P(None, "dp", None),
        P(),
        P(),
    )
    return jax.shard_map(
        shards,
        mesh=mesh,
        in_specs=placed,
        out_specs=(P(None, None, "mp"), P(None, "dp", None), P(None, "dp", None)),
        check_vma=False,
    )
```

```python
import functools
import math

import jax
import jax.numpy as jnp
from jax import lax
from jax.experimental import pallas as pl
from jax.experimental.pallas import tpu as pltpu
from jax.sharding import PartitionSpec as P

PRIME = 65521
CUT = 46000
F32 = jnp.float32
BF16 = jnp.bfloat16
BOTH = ("dp", "mp")
NT = (((1,), (1,)), ((), ()))
TN = (((0,), (0,)), ((), ()))
HIGHEST = lax.Precision.HIGHEST


FOUR = range(4)
TWO = range(2)


def device(z, x, core, y):
    return ((z % 4 * 4 + x) * 2 + core) * 16 + z // 4 * 4 + y


SLABS = [
    [device(2 * pair + odd, x, core, y) for odd in TWO for x in FOUR for y in FOUR for core in TWO]
    for pair in range(8)
]
LINES = [
    [device(2 * pair + odd, x, core, y) for pair in range(8)]
    for odd in TWO
    for x in FOUR
    for y in FOUR
    for core in TWO
]


def copy_index(z_lo, x, core):
    return (z_lo * 4 + x) * 2 + core


def swap(z, x, core):
    return [
        (copy_index(a, b, c), copy_index(a ^ z, b ^ x, c ^ core))
        for a in FOUR
        for b in FOUR
        for c in TWO
    ]


def below(values, bound):
    return jnp.where(values >= bound, values - bound, values)


def fold(values):
    return values - PRIME * (values >> 16)


def product(values):
    return below(values, CUT) * ((values >> 1) + 1)


def scrambled(values):
    return below(fold(fold(product(values) + 12345)), PRIME)


def row_keys(offset, rank_ids):
    return below(fold(rank_ids * 251 + offset * 3), PRIME)


def column_keys(offset, columns):
    return below(2 * scrambled(below(fold(columns * 7 + offset), PRIME)), PRIME)


def entries(keys, keys_later, columns2, spread):
    first = fold(product(below(keys + columns2, PRIME)))
    second = below(fold(first * 3 + keys_later), PRIME)
    last = fold(product(second) + 12345).astype(F32)
    whole = jnp.floor((last + 0.5) * (1.0 / PRIME))
    return (((last - 32760.0) - whole * float(PRIME)) * (spread / PRIME)).astype(BF16)


def project_kernel(
    seeds,
    old_seeds,
    grads_hbm,
    first_hbm,
    second_hbm,
    weights_hbm,
    proj_hbm,
    send,
    weights_out,
    grads,
    moments,
    proj,
    keys,
    keys_later,
    columns2,
    old_rows,
    grads_sems,
    moment_sems,
    weights_sem,
    proj_sems,
    *,
    spread,
):
    layers, rank, cols = proj.shape
    dp, mp = lax.axis_index("dp"), lax.axis_index("mp")
    tiles = cols // 128
    share = 64 // layers
    grads_in = [
        pltpu.make_async_copy(grads_hbm.at[0, layer], grads.at[layer], grads_sems.at[layer])
        for layer in range(layers)
    ]
    moments_in = [
        pltpu.make_async_copy(source, moments.at[which], moment_sems.at[which])
        for which, source in enumerate((first_hbm, second_hbm))
    ]
    weights_move = pltpu.make_async_copy(weights_hbm, weights_out, weights_sem)
    proj_out = [
        pltpu.make_async_copy(proj.at[layer], proj_hbm.at[layer], proj_sems.at[layer])
        for layer in range(layers)
    ]
    for copy in (*grads_in, *moments_in, weights_move):
        copy.start()

    def both_halves(eight):
        return jnp.concatenate([eight, eight], axis=0)

    lanes = lax.broadcasted_iota(jnp.int32, (8, cols), 1) + mp * cols
    row = lax.broadcasted_iota(jnp.int32, (rank, 128), 0)
    old_block = dp % (rank // 16)
    old_row = lax.broadcasted_iota(jnp.int32, (16, 128), 0) + old_block * 16
    for layer in range(layers):
        offset = lax.rem(old_seeds[layer], PRIME)
        mine = row_keys(offset, old_row)
        later = below(mine + 3 * 12345, PRIME)
        old_columns2 = column_keys(offset, lanes)
        for tile in range(tiles):
            cut = slice(tile * 128, tile * 128 + 128)
            old_rows[layer, :, cut] = entries(
                mine, later, both_halves(old_columns2[:, cut]), spread
            )
        offset = lax.rem(seeds[layer], PRIME)
        keys[layer] = row_keys(offset, row)
        keys_later[layer] = below(keys[layer] + 3 * 12345, PRIME)
        columns2[layer] = column_keys(offset, lanes)

    for layer in range(layers):

        def chunk(index, _, layer=layer):
            rows = pl.ds(pl.multiple_of(index * 16, 16), 16)
            mine, later = keys[layer, rows, :], keys_later[layer, rows, :]
            for tile in range(tiles):
                cut = slice(tile * 128, tile * 128 + 128)
                proj[layer, rows, cut] = entries(
                    mine, later, both_halves(columns2[layer, :, cut]), spread
                )
            return 0

        lax.fori_loop(0, rank // 16, chunk, 0, unroll=2)
        proj_out[layer].start()

    for copy in (*grads_in, *moments_in):
        copy.wait()
    y = mp % 4
    spot_row = lax.broadcasted_iota(jnp.int32, (16, rank), 0) + old_block * 16
    spot_lane = lax.broadcasted_iota(jnp.int32, (16, rank), 1)
    for layer in range(layers):
        group = slice(share * layer, share * layer + share)
        compressed = lax.dot_general(proj[layer], grads[layer], NT, preferred_element_type=F32)
        send[group, :, 0:rank] = compressed.reshape(share, 8, rank).astype(BF16)
        gram = lax.dot_general(proj[layer], old_rows[layer], NT, preferred_element_type=F32)
        mine_layer = dp // (rank // 16) == layer
        spot = jnp.where((spot_row == spot_lane) & mine_layer, 1.0, 0.0).astype(BF16)
        placed = jnp.dot(gram.astype(BF16), spot, preferred_element_type=F32)
        send[group, :, rank : 2 * rank] = placed.reshape(share, 8, rank).astype(BF16)
        moment = jnp.where(y < 2, moments[0, layer], moments[1, layer])
        half = jnp.where(y % 2 == 0, moment[:, 0:128], moment[:, 128:256])
        send[group, :, 2 * rank : 2 * rank + 128] = jnp.broadcast_to(
            half[None], (share, 8, 128)
        ).astype(BF16)
    for copy in (weights_move, *proj_out):
        copy.wait()


def summed(received, width):
    total = received[0, :, 0:width].astype(F32)
    for part in range(1, received.shape[0]):
        total = total + received[part, :, 0:width].astype(F32)
    return total


def sum_kernel(received, send, moments):
    send[...] = jnp.broadcast_to(summed(received, 512)[None], send.shape).astype(BF16)
    for chip in range(8):
        for y in FOUR:
            from_core = [received[(chip * 4 + y) * 2 + core, :, 512:640].astype(F32) for core in TWO]
            lanes = slice(y % 2 * 128, y % 2 * 128 + 128)
            moments[y // 2, chip * 16 : chip * 16 + 16, lanes] = jnp.concatenate(
                from_core, axis=0
            ).astype(BF16)


def join_kernel(*refs):
    *pieces, _, joined = refs
    for slot, piece in enumerate(pieces):
        joined[slot] = piece[...]


def moment_kernel(received, near, far, *refs):
    send = refs[-1]
    total = summed(received, 512)
    compressed, gram = total[:, 0:256], total[:, 256:512]
    upper = (lax.axis_index("dp") // 16) == 1

    def times(left, which):
        near_part, far_part = near[which].astype(F32), far[which].astype(F32)
        return jnp.concatenate(
            [
                lax.dot_general(
                    left, rows, NT, precision=HIGHEST, preferred_element_type=F32
                )
                for rows in (
                    jnp.where(upper, far_part, near_part),
                    jnp.where(upper, near_part, far_part),
                )
            ],
            axis=1,
        )

    first = 0.9 * times(gram, 0) + 0.1 * compressed
    second = 0.95 * times(gram * gram, 1) + 0.05 * compressed * compressed
    direction = first / (jnp.sqrt(second) + 1e-08)
    send[:, :, 0:256] = jnp.broadcast_to(direction[None], (64, 8, 256)).astype(BF16)
    mine = [jnp.where(upper, value[:, 128:256], value[:, 0:128]) for value in (first, second)]
    high = [value.astype(BF16).astype(F32) for value in mine]
    parts = high + [value - top for value, top in zip(mine, high)]
    lane = lax.broadcasted_iota(jnp.int32, (8, 128), 1)
    for quarter in FOUR:
        packed = pltpu.roll(parts[0], (128 - 32 * quarter) % 128, 1)
        for slot in (1, 2, 3):
            moved = pltpu.roll(parts[slot], (32 * slot - 32 * quarter) % 128, 1)
            packed = jnp.where(lane >= 32 * slot, moved, packed)
        send[16 * quarter : 16 * quarter + 16, :, 256:384] = jnp.broadcast_to(
            packed[None], (16, 8, 128)
        ).astype(BF16)


def update_kernel(received, proj, *refs):
    own, other = refs[0:4], refs[4:8]
    new_weights, new_first, new_second, update = refs[8:]
    dp = lax.axis_index("dp")
    z, x, core = dp // 8, dp // 2 % 4, dp % 2
    direction = received[:, :, 0:256].astype(F32).reshape(256, 256).astype(BF16)
    update[...] = 0.5 * lax.dot_general(direction, proj[0], TN, preferred_element_type=F32)
    for x_bits in FOUR:
        for z_bits in FOUR:
            at = pl.multiple_of((z ^ z_bits) * 64 + (x ^ x_bits) * 16, 16)
            mine = own[x_bits][z_bits, 0].astype(F32)
            theirs = other[x_bits][z_bits, 0].astype(F32)
            low = jnp.where(core == 0, mine, theirs)
            high = jnp.where(core == 0, theirs, mine)
            block = jnp.concatenate([low, high], axis=0)
            new_weights[0, pl.ds(at, 16), :] = (block - update[pl.ds(at, 16), :]).astype(BF16)
    rows = lax.broadcasted_iota(jnp.int32, (16, 128), 0)
    lanes = lax.broadcasted_iota(jnp.int32, (16, 128), 1)
    wanted = rows // 8 * 32 + x % 2 * 16 + core * 8 + rows % 8
    chosen = jnp.where(lanes % 64 == wanted, 1.0, 0.0).astype(BF16)
    moments = lax.dot_general(
        chosen,
        received[:, :, 256:384].astype(F32).reshape(256, 128).astype(BF16),
        NT,
        preferred_element_type=F32,
    )
    new_first[0] = moments[0:8]
    new_second[0] = moments[8:16]


def shards(grads, weights, first_moment, second_moment, old_seeds, new_seeds):
    layers, block, cols = weights.shape
    rank = first_moment.shape[2]
    spread = math.sqrt(12.0 / rank)
    smem = pl.BlockSpec(memory_space=pltpu.SMEM)
    vmem = pl.BlockSpec(memory_space=pltpu.VMEM)
    hbm = pl.BlockSpec(memory_space=pltpu.HBM)
    anywhere = pl.BlockSpec(memory_space=pl.ANY)
    roomy = pltpu.CompilerParams(vmem_limit_bytes=251 * 2**18)
    small = pltpu.CompilerParams(vmem_limit_bytes=8 * 2**20)

    proj, send, weights = pl.pallas_call(
        functools.partial(project_kernel, spread=spread),
        in_specs=[smem, smem, hbm, hbm, hbm, hbm],
        out_specs=[hbm, vmem, hbm],
        out_shape=[
            jax.ShapeDtypeStruct((layers, rank, cols), BF16),
            jax.ShapeDtypeStruct((64, 8, 640), BF16),
            jax.ShapeDtypeStruct(weights.shape, BF16),
        ],
        scratch_shapes=[
            pltpu.VMEM((layers, rank, cols), BF16),
            pltpu.VMEM((2, layers, block, rank), F32),
            pltpu.VMEM((layers, rank, cols), BF16),
            pltpu.VMEM((layers, rank, 128), jnp.int32),
            pltpu.VMEM((layers, rank, 128), jnp.int32),
            pltpu.VMEM((layers, 8, cols), jnp.int32),
            pltpu.VMEM((layers, 16, cols), BF16),
            pltpu.SemaphoreType.DMA((layers,)),
            pltpu.SemaphoreType.DMA((2,)),
            pltpu.SemaphoreType.DMA(()),
            pltpu.SemaphoreType.DMA((layers,)),
        ],
        compiler_params=roomy,
        cost_estimate=pl.CostEstimate(
            flops=8 * 10**9, bytes_accessed=6 * 10**6, transcendentals=0
        ),
        name="project",
    )(new_seeds, old_seeds, grads, first_moment, second_moment, weights)

    received = lax.all_to_all(send, BOTH, 0, 0, axis_index_groups=SLABS, tiled=True)
    column = [weights] + [lax.ppermute(weights, "dp", swap(bits, 0, 0)) for bits in (1, 2, 3)]
    send, near = pl.pallas_call(
        sum_kernel,
        in_specs=[vmem],
        out_specs=[vmem, vmem],
        out_shape=[
            jax.ShapeDtypeStruct((8, 8, 2 * rank), BF16),
            jax.ShapeDtypeStruct((2, rank // 2, rank), BF16),
        ],
        compiler_params=small,
        name="slab_sum",
    )(received)
    received = lax.all_to_all(send, BOTH, 0, 0, axis_index_groups=LINES, tiled=True)
    far = lax.ppermute(near, "dp", swap(2, 0, 0))
    column = pl.pallas_call(
        join_kernel,
        in_specs=[vmem] * 5,
        out_specs=vmem,
        out_shape=jax.ShapeDtypeStruct((4, *weights.shape), BF16),
        compiler_params=small,
        name="join",
    )(*column, near)
    own = [column] + [lax.ppermute(column, "dp", swap(0, bits, 0)) for bits in (1, 2, 3)]
    send = pl.pallas_call(
        moment_kernel,
        in_specs=[vmem] * 6,
        out_specs=vmem,
        out_shape=jax.ShapeDtypeStruct((64, 8, 384), BF16),
        compiler_params=small,
        name="moment",
    )(received, near, far, *own[1:])
    received = lax.all_to_all(send, BOTH, 0, 0, axis_index_groups=SLABS, tiled=True)
    other = [lax.ppermute(piece, "dp", swap(0, 0, 1)) for piece in own]

    whole = pl.BlockSpec((1, rank, cols), lambda layer: (layer, 0, 0))
    piece = pl.BlockSpec((4, 1, block, cols), lambda layer: (0, layer, 0, 0))
    rows = pl.BlockSpec((1, block, rank), lambda layer: (layer, 0, 0))
    return pl.pallas_call(
        update_kernel,
        grid=(layers,),
        in_specs=[
            pl.BlockSpec((64 // layers, 8, 384), lambda layer: (layer, 0, 0)),
            whole,
        ]
        + [piece] * 8,
        out_specs=[whole, rows, rows],
        out_shape=[
            jax.ShapeDtypeStruct((layers, rank, cols), BF16),
            jax.ShapeDtypeStruct((layers, block, rank), F32),
            jax.ShapeDtypeStruct((layers, block, rank), F32),
        ],
        scratch_shapes=[pltpu.VMEM((rank, cols), F32)],
        compiler_params=pltpu.CompilerParams(vmem_limit_bytes=51 * 2**20),
        name="update",
    )(received, proj, *own, *other)


def solution(mesh):
    placed = (
        P("dp", None, None, "mp"),
        P(None, "dp", "mp"),
        P(None, "dp", None),
        P(None, "dp", None),
        P(),
        P(),
    )
    return jax.shard_map(
        shards,
        mesh=mesh,
        in_specs=placed,
        out_specs=(P(None, None, "mp"), P(None, "dp", None), P(None, "dp", None)),
        check_vma=False,
    )
```

```python
import functools
import math

import jax
import jax.numpy as jnp
from jax import lax
from jax.experimental import pallas as pl
from jax.experimental.pallas import tpu as pltpu
from jax.sharding import PartitionSpec as P

PRIME = 65521
CUT = 46000
F32 = jnp.float32
BF16 = jnp.bfloat16
BOTH = ("dp", "mp")
NT = (((1,), (1,)), ((), ()))
TN = (((0,), (0,)), ((), ()))
HIGHEST = lax.Precision.HIGHEST


FOUR = range(4)
TWO = range(2)


def device(z, x, core, y):
    return ((z % 4 * 4 + x) * 2 + core) * 16 + z // 4 * 4 + y


SLABS = [
    [device(2 * pair + odd, x, core, y) for odd in TWO for x in FOUR for y in FOUR for core in TWO]
    for pair in range(8)
]
LINES = [
    [device(2 * pair + odd, x, core, y) for pair in range(8)]
    for odd in TWO
    for x in FOUR
    for y in FOUR
    for core in TWO
]


def copy_index(z_lo, x, core):
    return (z_lo * 4 + x) * 2 + core


def swap(z, x, core):
    return [
        (copy_index(a, b, c), copy_index(a ^ z, b ^ x, c ^ core))
        for a in FOUR
        for b in FOUR
        for c in TWO
    ]


def below(values, bound):
    return jnp.where(values >= bound, values - bound, values)


def fold(values):
    return values - PRIME * (values >> 16)


def product(values):
    return below(values, CUT) * ((values >> 1) + 1)


def scrambled(values):
    return below(fold(fold(product(values) + 12345)), PRIME)


def row_keys(offset, rank_ids):
    return below(fold(rank_ids * 251 + offset * 3), PRIME)


def column_keys(offset, columns):
    return below(2 * scrambled(below(fold(columns * 7 + offset), PRIME)), PRIME)


def entries(keys, keys_later, columns2, spread):
    first = fold(product(below(keys + columns2, PRIME)))
    second = below(fold(first * 3 + keys_later), PRIME)
    last = fold(product(second) + 12345).astype(F32)
    whole = jnp.floor((last + 0.5) * (1.0 / PRIME))
    return (((last - 32760.0) - whole * float(PRIME)) * (spread / PRIME)).astype(BF16)


def project_kernel(
    seeds,
    old_seeds,
    grads_hbm,
    first_hbm,
    second_hbm,
    weights_hbm,
    proj_hbm,
    send,
    weights_out,
    grads,
    moments,
    proj,
    keys,
    keys_later,
    columns2,
    old_rows,
    grads_sems,
    moment_sems,
    weights_sem,
    proj_sems,
    *,
    spread,
):
    layers, rank, cols = proj.shape
    dp, mp = lax.axis_index("dp"), lax.axis_index("mp")
    tiles = cols // 128
    share = 64 // layers
    grads_in = [
        pltpu.make_async_copy(grads_hbm.at[0, layer], grads.at[layer], grads_sems.at[layer])
        for layer in range(layers)
    ]
    moments_in = [
        pltpu.make_async_copy(source, moments.at[which], moment_sems.at[which])
        for which, source in enumerate((first_hbm, second_hbm))
    ]
    weights_move = pltpu.make_async_copy(weights_hbm, weights_out, weights_sem)
    proj_out = [
        pltpu.make_async_copy(proj.at[layer], proj_hbm.at[layer], proj_sems.at[layer])
        for layer in range(layers)
    ]
    for copy in (*grads_in, *moments_in, weights_move):
        copy.start()

    def both_halves(eight):
        return jnp.concatenate([eight, eight], axis=0)

    lanes = lax.broadcasted_iota(jnp.int32, (8, cols), 1) + mp * cols
    row = lax.broadcasted_iota(jnp.int32, (rank, 128), 0)
    old_block = dp % (rank // 16)
    old_row = lax.broadcasted_iota(jnp.int32, (16, 128), 0) + old_block * 16
    for layer in range(layers):
        offset = lax.rem(old_seeds[layer], PRIME)
        mine = row_keys(offset, old_row)
        later = below(mine + 3 * 12345, PRIME)
        old_columns2 = column_keys(offset, lanes)
        for tile in range(tiles):
            cut = slice(tile * 128, tile * 128 + 128)
            old_rows[layer, :, cut] = entries(
                mine, later, both_halves(old_columns2[:, cut]), spread
            )
        offset = lax.rem(seeds[layer], PRIME)
        keys[layer] = row_keys(offset, row)
        keys_later[layer] = below(keys[layer] + 3 * 12345, PRIME)
        columns2[layer] = column_keys(offset, lanes)

    for layer in range(layers):

        def chunk(index, _, layer=layer):
            rows = pl.ds(pl.multiple_of(index * 16, 16), 16)
            mine, later = keys[layer, rows, :], keys_later[layer, rows, :]
            for tile in range(tiles):
                cut = slice(tile * 128, tile * 128 + 128)
                proj[layer, rows, cut] = entries(
                    mine, later, both_halves(columns2[layer, :, cut]), spread
                )
            return 0

        lax.fori_loop(0, rank // 16, chunk, 0, unroll=2)
        proj_out[layer].start()

    for copy in (*grads_in, *moments_in):
        copy.wait()
    y = mp % 4
    spot_row = lax.broadcasted_iota(jnp.int32, (16, rank), 0) + old_block * 16
    spot_lane = lax.broadcasted_iota(jnp.int32, (16, rank), 1)
    for layer in range(layers):
        group = slice(share * layer, share * layer + share)
        compressed = lax.dot_general(proj[layer], grads[layer], NT, preferred_element_type=F32)
        send[group, :, 0:rank] = compressed.reshape(share, 8, rank).astype(BF16)
        gram = lax.dot_general(proj[layer], old_rows[layer], NT, preferred_element_type=F32)
        mine_layer = dp // (rank // 16) == layer
        spot = jnp.where((spot_row == spot_lane) & mine_layer, 1.0, 0.0).astype(BF16)
        placed = jnp.dot(gram.astype(BF16), spot, preferred_element_type=F32)
        send[group, :, rank : 2 * rank] = placed.reshape(share, 8, rank).astype(BF16)
        moment = jnp.where(y < 2, moments[0, layer], moments[1, layer])
        half = jnp.where(y % 2 == 0, moment[:, 0:128], moment[:, 128:256])
        send[group, :, 2 * rank : 2 * rank + 128] = jnp.broadcast_to(
            half[None], (share, 8, 128)
        ).astype(BF16)
    for copy in (weights_move, *proj_out):
        copy.wait()


def summed(received, width):
    total = received[0, :, 0:width].astype(F32)
    for part in range(1, received.shape[0]):
        total = total + received[part, :, 0:width].astype(F32)
    return total


def sum_kernel(received, send, moments):
    send[...] = jnp.broadcast_to(summed(received, 512)[None], send.shape).astype(BF16)
    for chip in range(8):
        for y in FOUR:
            from_core = [received[(chip * 4 + y) * 2 + core, :, 512:640].astype(F32) for core in TWO]
            lanes = slice(y % 2 * 128, y % 2 * 128 + 128)
            moments[y // 2, chip * 16 : chip * 16 + 16, lanes] = jnp.concatenate(
                from_core, axis=0
            ).astype(BF16)


def join_kernel(*refs):
    *pieces, _, joined = refs
    for slot, piece in enumerate(pieces):
        joined[slot] = piece[...]


def moment_kernel(received, near, far, *refs):
    send = refs[-1]
    total = summed(received, 512)
    compressed, gram = total[:, 0:256], total[:, 256:512]
    upper = (lax.axis_index("dp") // 16) == 1

    def times(left, which):
        near_part, far_part = near[which].astype(F32), far[which].astype(F32)
        return jnp.concatenate(
            [
                lax.dot_general(
                    left, rows, NT, precision=HIGHEST, preferred_element_type=F32
                )
                for rows in (
                    jnp.where(upper, far_part, near_part),
                    jnp.where(upper, near_part, far_part),
                )
            ],
            axis=1,
        )

    first = 0.9 * times(gram, 0) + 0.1 * compressed
    second = 0.95 * times(gram * gram, 1) + 0.05 * compressed * compressed
    direction = first / (jnp.sqrt(second) + 1e-08)
    send[:, :, 0:256] = jnp.broadcast_to(direction[None], (64, 8, 256)).astype(BF16)
    mine = [jnp.where(upper, value[:, 128:256], value[:, 0:128]) for value in (first, second)]
    high = [value.astype(BF16).astype(F32) for value in mine]
    parts = high + [value - top for value, top in zip(mine, high)]
    lane = lax.broadcasted_iota(jnp.int32, (8, 128), 1)
    for quarter in FOUR:
        packed = pltpu.roll(parts[0], (128 - 32 * quarter) % 128, 1)
        for slot in (1, 2, 3):
            moved = pltpu.roll(parts[slot], (32 * slot - 32 * quarter) % 128, 1)
            packed = jnp.where(lane >= 32 * slot, moved, packed)
        send[16 * quarter : 16 * quarter + 16, :, 256:384] = jnp.broadcast_to(
            packed[None], (16, 8, 128)
        ).astype(BF16)


def update_kernel(received, proj, *refs):
    own, other = refs[0:4], refs[4:8]
    new_weights, new_first, new_second, update = refs[8:]
    dp = lax.axis_index("dp")
    z, x, core = dp // 8, dp // 2 % 4, dp % 2
    direction = received[:, :, 0:256].astype(F32).reshape(256, 256).astype(BF16)
    update[...] = 0.5 * lax.dot_general(direction, proj[0], TN, preferred_element_type=F32)
    for x_bits in FOUR:
        for z_bits in FOUR:
            at = pl.multiple_of((z ^ z_bits) * 64 + (x ^ x_bits) * 16, 16)
            mine = own[x_bits][z_bits, 0].astype(F32)
            theirs = other[x_bits][z_bits, 0].astype(F32)
            low = jnp.where(core == 0, mine, theirs)
            high = jnp.where(core == 0, theirs, mine)
            block = jnp.concatenate([low, high], axis=0)
            new_weights[0, pl.ds(at, 16), :] = (block - update[pl.ds(at, 16), :]).astype(BF16)
    rows = lax.broadcasted_iota(jnp.int32, (16, 128), 0)
    lanes = lax.broadcasted_iota(jnp.int32, (16, 128), 1)
    wanted = rows // 8 * 32 + x % 2 * 16 + core * 8 + rows % 8
    chosen = jnp.where(lanes % 64 == wanted, 1.0, 0.0).astype(BF16)
    moments = lax.dot_general(
        chosen,
        received[:, :, 256:384].astype(F32).reshape(256, 128).astype(BF16),
        NT,
        preferred_element_type=F32,
    )
    new_first[0] = moments[0:8]
    new_second[0] = moments[8:16]


def shards(grads, weights, first_moment, second_moment, old_seeds, new_seeds):
    layers, block, cols = weights.shape
    rank = first_moment.shape[2]
    spread = math.sqrt(12.0 / rank)
    smem = pl.BlockSpec(memory_space=pltpu.SMEM)
    vmem = pl.BlockSpec(memory_space=pltpu.VMEM)
    hbm = pl.BlockSpec(memory_space=pltpu.HBM)
    anywhere = pl.BlockSpec(memory_space=pl.ANY)
    roomy = pltpu.CompilerParams(vmem_limit_bytes=50 * 2**20)
    small = pltpu.CompilerParams(vmem_limit_bytes=8 * 2**20)

    proj, send, weights = pl.pallas_call(
        functools.partial(project_kernel, spread=spread),
        in_specs=[smem, smem, hbm, hbm, hbm, hbm],
        out_specs=[hbm, vmem, hbm],
        out_shape=[
            jax.ShapeDtypeStruct((layers, rank, cols), BF16),
            jax.ShapeDtypeStruct((64, 8, 640), BF16),
            jax.ShapeDtypeStruct(weights.shape, BF16),
        ],
        scratch_shapes=[
            pltpu.VMEM((layers, rank, cols), BF16),
            pltpu.VMEM((2, layers, block, rank), F32),
            pltpu.VMEM((layers, rank, cols), BF16),
            pltpu.VMEM((layers, rank, 128), jnp.int32),
            pltpu.VMEM((layers, rank, 128), jnp.int32),
            pltpu.VMEM((layers, 8, cols), jnp.int32),
            pltpu.VMEM((layers, 16, cols), BF16),
            pltpu.SemaphoreType.DMA((layers,)),
            pltpu.SemaphoreType.DMA((2,)),
            pltpu.SemaphoreType.DMA(()),
            pltpu.SemaphoreType.DMA((layers,)),
        ],
        compiler_params=roomy,
        cost_estimate=pl.CostEstimate(
            flops=8 * 10**9, bytes_accessed=6 * 10**6, transcendentals=0
        ),
        name="project",
    )(new_seeds, old_seeds, grads, first_moment, second_moment, weights)

    received = lax.all_to_all(send, BOTH, 0, 0, axis_index_groups=SLABS, tiled=True)
    column = [weights] + [lax.ppermute(weights, "dp", swap(bits, 0, 0)) for bits in (1, 2, 3)]
    send, near = pl.pallas_call(
        sum_kernel,
        in_specs=[vmem],
        out_specs=[vmem, vmem],
        out_shape=[
            jax.ShapeDtypeStruct((8, 8, 2 * rank), BF16),
            jax.ShapeDtypeStruct((2, rank // 2, rank), BF16),
        ],
        compiler_params=small,
        name="slab_sum",
    )(received)
    received = lax.all_to_all(send, BOTH, 0, 0, axis_index_groups=LINES, tiled=True)
    far = lax.ppermute(near, "dp", swap(2, 0, 0))
    column = pl.pallas_call(
        join_kernel,
        in_specs=[vmem] * 5,
        out_specs=vmem,
        out_shape=jax.ShapeDtypeStruct((4, *weights.shape), BF16),
        compiler_params=small,
        name="join",
    )(*column, near)
    own = [column] + [lax.ppermute(column, "dp", swap(0, bits, 0)) for bits in (1, 2, 3)]
    send = pl.pallas_call(
        moment_kernel,
        in_specs=[vmem] * 6,
        out_specs=vmem,
        out_shape=jax.ShapeDtypeStruct((64, 8, 384), BF16),
        compiler_params=small,
        name="moment",
    )(received, near, far, *own[1:])
    received = lax.all_to_all(send, BOTH, 0, 0, axis_index_groups=SLABS, tiled=True)
    other = [lax.ppermute(piece, "dp", swap(0, 0, 1)) for piece in own]

    whole = pl.BlockSpec((1, rank, cols), lambda layer: (layer, 0, 0))
    piece = pl.BlockSpec((4, 1, block, cols), lambda layer: (0, layer, 0, 0))
    rows = pl.BlockSpec((1, block, rank), lambda layer: (layer, 0, 0))
    return pl.pallas_call(
        update_kernel,
        grid=(layers,),
        in_specs=[
            pl.BlockSpec((64 // layers, 8, 384), lambda layer: (layer, 0, 0)),
            whole,
        ]
        + [piece] * 8,
        out_specs=[whole, rows, rows],
        out_shape=[
            jax.ShapeDtypeStruct((layers, rank, cols), BF16),
            jax.ShapeDtypeStruct((layers, block, rank), F32),
            jax.ShapeDtypeStruct((layers, block, rank), F32),
        ],
        scratch_shapes=[pltpu.VMEM((rank, cols), F32)],
        compiler_params=pltpu.CompilerParams(vmem_limit_bytes=51 * 2**20),
        name="update",
    )(received, proj, *own, *other)


def solution(mesh):
    placed = (
        P("dp", None, None, "mp"),
        P(None, "dp", "mp"),
        P(None, "dp", None),
        P(None, "dp", None),
        P(),
        P(),
    )
    return jax.shard_map(
        shards,
        mesh=mesh,
        in_specs=placed,
        out_specs=(P(None, None, "mp"), P(None, "dp", None), P(None, "dp", None)),
        check_vma=False,
    )
```
